32 devices in a mesh: groups: 2 (over x), tile: 16 (over z, y, core).
Axes of the slice: x: 2, y: 2, z: 4, core: 2. Of those that a mesh axis runs over, the one named last changes fastest.
Arguments:
- image: float32 [4, 768, 4096], P(None, ('groups', 'tile')), parts along dimension 1, may hold values from -6 to 6
- inv_var: float32 [4, 768, 4096], P(None, ('groups', 'tile')), parts along dimension 1, may hold values from 0.25 to 4
- shift: float32 [8, 2], P('groups'), parts along dimension 0, may hold values from -0.5 to 0.5
- col_offset: int32 [8], P('groups'), parts along dimension 0, may hold values from -8 to 8
- psf_rows: float32 [8, 3, 41], P('groups'), parts along dimension 0, may hold values from -1 to 1
- psf_cols: float32 [8, 3, 41], P('groups'), parts along dimension 0, may hold values from -0.5 to 0.5
- placement: int32 [4096, 1], P(('groups', 'tile')), parts along dimension 0, may hold values from 0 to 15; in each aligned block of 128 rows (0 to 127, 128 to 255, ...) at most 16 rows name the same one
Outputs:
- matched: bfloat16 [4, 768, 4096], P(None, ('groups', 'tile')), parts along dimension 1
- coadd: float32 [32, 24, 128], P(('groups', 'tile')), parts along dimension 0
The draws below stay inside these ranges and needn't reach their ends.
There are 2 independent parts, one for each index of `groups`. The reference program is written for one: setup_inputs(seed, part) draws one part's arguments, and reference() takes and returns one part's arrays. A program takes and returns all parts, laid end to end along the dimension named above; each array names one. Nothing has to cross between parts.
Inputs may be any that keep to these rules, and one draw needn't show every extreme that they name: `placement`: every patch receives at least one piece; within the pieces of one device no patch is named more than 16 times, a bound that some block reaches.
All inputs are finite; a program needn't handle non-finite values.
Results may differ from the reference program's by a relative error of at most 0.001.
Values sent between devices are 32-bit elements; how exact they have to be, the bound alone decides.
A program may use at most 192 MiB of HBM per device.

```python
import math
import jax
import jax.numpy as jnp
import numpy as np
from jax import lax

RD = 24
V = 4
W = 4096
K = 3
PC = 128
ROWS = 384
PIECES = 2048
CAP = 16
N_TILE = 16


def touch_ends(values, own_key, smallest, largest):
    shape = values.shape
    spot = [jax.random.randint(jax.random.fold_in(own_key, axis), (), 0, shape[axis]) for axis in range(len(shape))]
    values = values.at[tuple(spot)].set(smallest)
    longest = shape.index(max(shape))
    spot[longest] = (spot[longest] + 1) % shape[longest]
    return values.at[tuple(spot)].set(largest)


def shard_levels(own_key, dims, cuts, low, largest):
    def one(axis_at, shards_of):
        heights = jax.random.uniform(jax.random.fold_in(jax.random.fold_in(own_key, 6), axis_at), (shards_of,), jnp.float32, low / len(cuts), largest / len(cuts))
        return jnp.repeat(jnp.exp(heights), dims[axis_at] // shards_of).reshape((-1,) + (1,) * (len(dims) - axis_at - 1))

    gain = one(*cuts[0])
    for cut in cuts[1:]:
        gain = gain * one(*cut)
    return gain


def routed_block(stream_key, own, number, rows, count, top, bound, slope):
    ranking = jax.random.permutation(stream_key, count)
    packed, common = portions_of(count, rows * top, bound, slope, True), portions_of(count, rows * top, bound, slope, False)
    places = jnp.arange(count)

    def named(sizes, turn):
        used = int((sizes > 0).sum())
        fixed = max(1, used // 4)
        moved = fixed + (places - fixed + turn * (used - fixed)) % max(1, count - fixed)
        return jnp.zeros((count,), jnp.int32).at[ranking[jnp.where(places < fixed, places, moved)]].set(jnp.asarray(sizes, jnp.int32))

    sizes = jnp.where(number % 4 == 0, named(packed, number // 4), named(common, number - number // 4 - 1))
    mixed = jax.random.permutation(jax.random.fold_in(own, 3), count)
    source_of, sink = mixed[0:count // 2 * 2:2], mixed[1:count // 2 * 2:2]
    margin = jnp.minimum(sizes[source_of] - 1, bound - sizes[sink]) // 2
    margin = jnp.where((source_of == ranking[0]) | (sink == ranking[0]) | (sizes[sink] == 0), 0, jnp.maximum(margin, 0))
    moved = jax.random.randint(jax.random.fold_in(own, 4), (count // 2,), 0, 1 << 20) % (margin + 1)
    sizes = sizes.at[source_of].add(-moved).at[sink].add(moved)
    members = jnp.searchsorted(jnp.cumsum(sizes), jnp.arange(rows * top), side="right").astype(jnp.int32)
    grid = members.reshape(top, rows).T
    grid = grid[jax.random.permutation(jax.random.fold_in(own, 1), rows)]
    turn = jax.random.randint(jax.random.fold_in(own, 2), (rows, 1), 0, top)
    return jnp.take_along_axis(grid, (jnp.arange(top)[None, :] + turn) % top, axis=1)


def portions_of(amount, total, reach, slope, full):
    weights = [(1 << 20) // math.isqrt(rank ** slope) + 1 for rank in range(1, amount + 1)]
    largest = reach if full else min(reach, max(-(-total // amount), total * weights[0] // sum(weights)))
    least = 1 if total - largest >= amount - 1 else 0
    holding, spare = [largest] + [least] * (amount - 1), total - largest - least * (amount - 1)
    while spare > 0:
        candidates = [i for i in range(1, amount) if holding[i] < largest] or [i for i in range(1, amount) if holding[i] < reach]
        whole, remaining = sum([weights[i] for i in candidates]), spare
        for i in candidates:
            addition = min(reach - holding[i], max(1, remaining * weights[i] // whole), spare)
            holding[i] = holding[i] + addition
            spare = spare - addition
    return np.array(holding)


def gaussian(key, extent, scale, bound, split=(), kind=jnp.bfloat16):
    result = jax.random.normal(key, extent, jnp.float32) * scale
    if len(split) > 0:
        result = shard_levels(key, extent, split, -0.22, 0.18) * result
    return jnp.clip(result, min=-bound, max=bound).astype(kind)


def setup_inputs(seed: int = 0, part: int = 0) -> dict:
    keys = jax.random.split(jax.random.key(seed), 8)
    own_keys = jax.random.split(jax.random.fold_in(keys[7], part), 8)
    image = gaussian(own_keys[0], (V, ROWS, W), 1.0, 6.0, ((1, 16),), jnp.float32)
    inv_var = jnp.clip(jnp.exp(math.log(4.0) - 2.7725887 * jax.random.uniform(own_keys[1], (V, ROWS, W), jnp.float32) ** shard_levels(own_keys[1], (V, ROWS, W), ((1, 16),), -0.2, 0.2)), 0.25, 4.0)
    shift = jnp.clip(jax.random.uniform(own_keys[2], (V, 2), jnp.float32, -0.5, 0.5), -0.5, 0.5)
    col_offset = touch_ends(jax.random.randint(own_keys[3], (V,), -8, 9), jax.random.fold_in(own_keys[3], 1), -8, 8).astype(jnp.int32)
    psf_rows = gaussian(own_keys[4], (V, K, 41), 41 ** -0.5, 1.0, (), jnp.float32)
    psf_cols = gaussian(own_keys[5], (V, K, 41), (41 * K) ** -0.5, 0.5, (), jnp.float32)
    placement_keys = jax.random.split(jax.random.fold_in(own_keys[6], 1), PIECES // (V * (W // PC)))
    placement_turns = jax.random.permutation(jax.random.fold_in(own_keys[6], 3), PIECES // (V * (W // PC)))
    placement = jax.vmap(lambda own, number: routed_block(jax.random.fold_in(own_keys[6], 2), own, number, V * (W // PC), N_TILE, 1, CAP, 2))(placement_keys, placement_turns).reshape((PIECES, 1))
    return dict(image=image, inv_var=inv_var, shift=shift, col_offset=col_offset, psf_rows=psf_rows, psf_cols=psf_cols, placement=placement)


def lanczos(values):
    return jnp.where(jnp.abs(values) < 3.0, jnp.sinc(values) * jnp.sinc(values / 3.0), 0.0)


def tap_weights(fraction):
    places = jnp.arange(-3, 4).astype(jnp.float32)
    weights = lanczos(places[None, :] + fraction[:, None])
    return weights / jnp.sum(weights, axis=1, keepdims=True)


def warp(extended, shift, col_offset):
    height = extended.shape[1] - 6
    width = extended.shape[2]
    row_weight = tap_weights(shift[:, 0])
    col_weight = tap_weights(shift[:, 1])
    shifted = jnp.zeros((extended.shape[0], height, width), jnp.float32)
    for place in range(-3, 4):
        shifted = shifted + row_weight[:, place + 3, None, None] * extended[:, 3 - place:3 - place + height]
    padded = jnp.pad(shifted, ((0, 0), (0, 0), (11, 11)))

    def one_visit(plane, weights, offset):
        total = jnp.zeros((height, width), jnp.float32)
        for place in range(-3, 4):
            start = (11 - offset - place).astype(jnp.int32)
            total = total + weights[place + 3] * lax.dynamic_slice_in_dim(plane, start, width, 1)
        return total

    return jax.vmap(one_visit)(padded, col_weight, col_offset)


def match_psf(warped, psf_rows, psf_cols):
    height = warped.shape[1]
    width = warped.shape[2]
    padded_rows = jnp.pad(warped, ((0, 0), (20, 20), (0, 0)))
    matched = jnp.zeros(warped.shape, jnp.float32)
    for basis in range(psf_rows.shape[1]):
        along = jnp.zeros(warped.shape, jnp.float32)
        for place in range(41):
            along = along + psf_rows[:, basis, place, None, None] * padded_rows[:, 40 - place:40 - place + height]
        padded_cols = jnp.pad(along, ((0, 0), (0, 0), (20, 20)))
        for place in range(41):
            matched = matched + psf_cols[:, basis, place, None, None] * padded_cols[:, :, 40 - place:40 - place + width]
    return matched


def reference(image, inv_var, shift, col_offset, psf_rows, psf_cols, placement):
    warped = warp(jnp.pad(image, ((0, 0), (3, 3), (0, 0))), shift, col_offset)
    matched = match_psf(warped, psf_rows, psf_cols)
    visits = image.shape[0]
    width = image.shape[2]
    pieces = width // PC
    labels = placement.reshape(N_TILE, visits, pieces)
    owners = jnp.arange(N_TILE, dtype=jnp.int32)
    onehot = (labels[None] == owners[:, None, None, None]).astype(jnp.float32)
    weighted = (inv_var * matched).reshape(visits, N_TILE, RD, pieces, PC)
    weights = inv_var.reshape(visits, N_TILE, RD, pieces, PC)
    numer = jnp.einsum("pdvc,vdrcx->prx", onehot, weighted, precision=lax.Precision.HIGHEST)
    denom = jnp.einsum("pdvc,vdrcx->prx", onehot, weights, precision=lax.Precision.HIGHEST)
    return matched.astype(jnp.bfloat16), numer / jnp.maximum(denom, 1.0)
```

```python
import functools

import jax
import jax.numpy as jnp
from jax import lax
from jax.experimental import pallas as pl
from jax.experimental.pallas import tpu as pltpu
from jax.sharding import PartitionSpec as P

PC = 128
LEAD = 20
BF = jnp.bfloat16
F32 = jnp.float32


def lanczos(values):
    return jnp.where(jnp.abs(values) < 3.0, jnp.sinc(values) * jnp.sinc(values / 3.0), 0.0)


def tap_weights(fraction):
    places = jnp.arange(-3, 4).astype(F32)
    weights = lanczos(places[None, :] + fraction[:, None])
    return weights / jnp.sum(weights, axis=1, keepdims=True)


def two_terms(x):
    high = x.astype(BF)
    return high, (x - high.astype(F32)).astype(BF)


def rounded_terms(x):
    high = lax.reduce_precision(x, exponent_bits=8, mantissa_bits=7)
    return high.astype(BF), (x - high).astype(BF)


def pick(weights, index):
    total = 0.0
    for t in range(weights.shape[1]):
        w = weights[:, t].reshape((-1,) + (1,) * (index.ndim - 1))
        total = total + jnp.where(index == t, w, 0.0)
    return total


def row_operator(row_tap, psf_rows, height, me, n):
    visits, terms, _ = psf_rows.shape
    i = jnp.arange(height, dtype=jnp.int32)[:, None, None]
    m = jnp.arange(height + 40, dtype=jnp.int32)[None, :, None]
    select = (i - m + 40 == jnp.arange(41, dtype=jnp.int32)[None, None, :]).astype(F32)
    band = jnp.einsum("vka,ima->vkim", psf_rows, select, precision=lax.Precision.HIGHEST)
    mi = jnp.arange(height + 40, dtype=jnp.int32)[:, None]
    ri = jnp.arange(3 * height, dtype=jnp.int32)[None, :]
    taps = pick(row_tap, (mi - ri + height - LEAD + 3)[None])
    row = me * height + mi - LEAD
    taps = jnp.where((row >= 0) & (row < n * height), taps, 0.0)
    full = jnp.einsum("vkim,vmr->vkir", band, taps, precision=lax.Precision.HIGHEST)
    full = full.reshape(visits, terms * height, 3 * height)
    high, low = rounded_terms(full)
    stacked = jnp.concatenate([high, high, low], axis=2)
    rows = -(-stacked.shape[1] // 16) * 16
    depth = -(-stacked.shape[2] // 256) * 256
    return jnp.pad(
        stacked, ((0, 0), (0, rows - stacked.shape[1]), (0, depth - stacked.shape[2]))
    )


def edge_operator(col_tap, col_offset, psf_cols):
    visits, terms, _ = psf_cols.shape
    m = jnp.arange(PC, dtype=jnp.int32)[:, None]
    j = jnp.arange(LEAD, dtype=jnp.int32)[None, :]
    place = jnp.stack([j - LEAD - m, PC + j - m])[None] - col_offset[:, None, None, None]
    taps = pick(col_tap, place + 3)
    jj = jnp.arange(LEAD, dtype=jnp.int32)[:, None]
    o = jnp.arange(PC, dtype=jnp.int32)[None, :]
    index = jnp.stack([o - jj + 40, o - PC - jj + 20])
    select = (index[..., None] == jnp.arange(41, dtype=jnp.int32)).astype(F32)
    psf = jnp.einsum("vkb,ejob->vkejo", psf_cols, select, precision=lax.Precision.HIGHEST)
    full = jnp.einsum("vemj,vkejo->vekmo", taps, psf, precision=lax.Precision.HIGHEST)
    high, low = rounded_terms(full.reshape(visits, 2, terms * PC, PC))
    return jnp.concatenate([high, low], axis=3)


def band_kernel(terms, c_ref, out_ref):
    for k in range(terms):
        row = jnp.broadcast_to(c_ref[0, k : k + 1, :], (PC, 2 * PC))
        turned = pltpu.roll(row, 0, 1, stride=1, stride_axis=0)
        m = lax.broadcasted_iota(jnp.int32, (PC, PC), 0)
        o = lax.broadcasted_iota(jnp.int32, (PC, PC), 1)
        far = turned[:, PC:]
        for d, part in enumerate(
            [jnp.where(o < m, far, 0.0), turned[:, :PC], jnp.where(o > m, far, 0.0)]
        ):
            high = part.astype(BF)
            low = (part - high.astype(F32)).astype(BF)
            start = (3 * k + d) * PC
            out_ref[0, start : start + PC, :PC] = high
            out_ref[0, start : start + PC, PC:] = low


def col_operator(col_tap, col_offset, psf_cols):
    visits, terms, _ = psf_cols.shape
    b = jnp.arange(41, dtype=jnp.int32)[:, None]
    lane = jnp.arange(2 * PC, dtype=jnp.int32)[None, :]
    signed = jnp.where(lane < PC, lane, lane - 2 * PC)
    spread = pick(col_tap, (signed - b + LEAD + 3)[None] - col_offset[:, None, None])
    line = jnp.einsum("vkb,vbl->vkl", psf_cols, spread, precision=lax.Precision.HIGHEST)
    return pl.pallas_call(
        functools.partial(band_kernel, terms),
        grid=(visits,),
        in_specs=[pl.BlockSpec((1, terms, 2 * PC), lambda v: (v, 0, 0))],
        out_specs=pl.BlockSpec((1, terms * 3 * PC, 2 * PC), lambda v: (v, 0, 0)),
        out_shape=jax.ShapeDtypeStruct((visits, terms * 3 * PC, 2 * PC), BF),
    )(line)


def split_dot(x, w_ref):
    high, low = two_terms(x)
    wide = jnp.dot(high, w_ref[...], preferred_element_type=F32)
    narrow = jnp.dot(low, w_ref[:, :PC], preferred_element_type=F32)
    return wide[:, :PC] + wide[:, PC:] + narrow


def main_kernel(
    n, terms, image, inv_var, rows_op, cols_op, edge_op, hot, out_m, out_c,
    halo, lines, block, sums, got, halo_send, halo_recv, sum_send, sum_recv,
):
    visits, height, width = image.shape
    pieces = width // PC
    me = lax.axis_index("tile")

    barrier = pltpu.get_barrier_semaphore()

    def greet(d, carry):
        pl.semaphore_signal(
            barrier, inc=1, device_id={"tile": lax.rem(me + d, n)},
            device_id_type=pl.DeviceIdType.MESH,
        )
        return carry

    lax.fori_loop(1, n, greet, 0)
    pl.semaphore_wait(barrier, n - 1)

    def halo_copy(v, side):
        other = me + 1 if side == 0 else me - 1
        return pltpu.make_async_remote_copy(
            src_ref=image.at[v], dst_ref=halo.at[side, v],
            send_sem=halo_send.at[side, v], recv_sem=halo_recv.at[side, v],
            device_id={"tile": other}, device_id_type=pl.DeviceIdType.MESH,
        )

    for v in range(visits):
        @pl.when(me < n - 1)
        def _():
            halo_copy(v, 0).start()

        @pl.when(me > 0)
        def _():
            halo_copy(v, 1).start()

    @pl.when(me == 0)
    def _():
        halo[0] = jnp.zeros_like(halo[0])

    @pl.when(me == n - 1)
    def _():
        halo[1] = jnp.zeros_like(halo[1])

    def add_up(v, which, first):
        def owner(p, carry):
            total = jnp.zeros((height, PC), F32) if first else sums[which, p]
            for c in range(pieces):
                total = total + hot[(v * pieces + c) * n + p] * block[c]
            sums[which, p] = total
            return carry

        lax.fori_loop(0, n, owner, 0)

    def sum_copy(which, d):
        return pltpu.make_async_remote_copy(
            src_ref=sums.at[which, lax.rem(me + d, n)], dst_ref=got.at[which, me],
            send_sem=sum_send.at[which, d], recv_sem=sum_recv.at[which, me],
            device_id={"tile": lax.rem(me + d, n)}, device_id_type=pl.DeviceIdType.MESH,
        )

    def send_sums(which):
        def one(d, carry):
            sum_copy(which, d).start()
            return carry

        lax.fori_loop(1, n, one, 0)

    for v in range(visits):
        for c in range(pieces):
            block[c] = inv_var[v, :, c * PC : (c + 1) * PC]
        add_up(v, 1, v == 0)
    send_sums(1)

    for k in range(terms):
        lines[k, 0] = jnp.zeros((height, PC), F32)
        lines[k, pieces + 1] = jnp.zeros((height, PC), F32)

    depth = rows_op.shape[2]
    step = 4
    for v in range(visits):
        @pl.when(me > 0)
        def _():
            pltpu.make_async_copy(image.at[v], halo.at[0, v], halo_recv.at[0, v]).wait()

        @pl.when(me < n - 1)
        def _():
            pltpu.make_async_copy(image.at[v], halo.at[1, v], halo_recv.at[1, v]).wait()

        def rows_stage(q, carry):
            cols = pl.ds(pl.multiple_of(q * (step * PC), step * PC), step * PC)
            x = jnp.concatenate([halo[0, v, :, cols], image[v, :, cols], halo[1, v, :, cols]], 0)
            high = x.astype(BF).astype(F32)
            rest = jnp.zeros((depth - 9 * height, step * PC), F32)
            stacked = jnp.concatenate([high, x - high, high, rest], 0).astype(BF)
            y = jnp.dot(rows_op[v], stacked, preferred_element_type=F32)
            for k in range(terms):
                for s in range(step):
                    lines[k, q * step + s + 1] = y[
                        k * height : (k + 1) * height, s * PC : (s + 1) * PC
                    ]
            return carry

        lax.fori_loop(0, pieces // step, rows_stage, 0)

        half = pieces // 2

        def cols_stage(q, carry):
            parts = [
                lines[k, pl.ds(q * half + d, half)].reshape(half * height, PC)
                for k in range(terms)
                for d in range(3)
            ]
            res = split_dot(jnp.concatenate(parts, 1), cols_op.at[v])
            block[pl.ds(q * half, half)] = res.reshape(half, height, PC)
            return carry

        lax.fori_loop(0, 2, cols_stage, 0)
        for e, c in ((0, 0), (1, pieces - 1)):
            x = jnp.concatenate([lines[k, c + 1] for k in range(terms)], 1)
            block[c] = block[c] - split_dot(x, edge_op.at[v, e])
        for c in range(pieces):
            cols = slice(c * PC, (c + 1) * PC)
            value = block[c]
            out_m[v, :, cols] = value.astype(BF)
            block[c] = value * inv_var[v, :, cols]
        add_up(v, 0, v == 0)
    send_sums(0)

    totals = []
    for which in (1, 0):
        def one(d, total):
            source = lax.rem(me + n - d, n)
            pltpu.make_async_copy(
                sums.at[which, 0], got.at[which, source], sum_recv.at[which, source]
            ).wait()
            return total + got[which, source]

        totals.append(lax.fori_loop(1, n, one, sums[which, me]))
    out_c[0] = totals[1] / jnp.maximum(totals[0], 1.0)

    for which in (0, 1):
        def done(d, carry):
            sum_copy(which, d).wait_send()
            return carry

        lax.fori_loop(1, n, done, 0)
    for v in range(visits):
        @pl.when(me < n - 1)
        def _():
            halo_copy(v, 0).wait_send()

        @pl.when(me > 0)
        def _():
            halo_copy(v, 1).wait_send()


def on_device(image, inv_var, shift, col_offset, psf_rows, psf_cols, placement):
    visits, height, width = image.shape
    n = lax.axis_size("tile")
    me = lax.axis_index("tile")
    terms = psf_rows.shape[1]
    pieces = width // PC
    row_tap = tap_weights(shift[:, 0])
    col_tap = tap_weights(shift[:, 1])
    rows_op = row_operator(row_tap, psf_rows, height, me, n)
    cols_op = col_operator(col_tap, col_offset, psf_cols)
    edge_op = edge_operator(col_tap, col_offset, psf_cols)
    hot = (placement == jnp.arange(n, dtype=jnp.int32)[None, :]).astype(F32).reshape(-1)
    vmem = pl.BlockSpec(memory_space=pltpu.VMEM)
    return pl.pallas_call(
        functools.partial(main_kernel, n, terms),
        out_shape=(
            jax.ShapeDtypeStruct((visits, height, width), BF),
            jax.ShapeDtypeStruct((1, height, PC), F32),
        ),
        in_specs=[vmem] * 5 + [pl.BlockSpec(memory_space=pltpu.SMEM)],
        out_specs=(vmem, vmem),
        scratch_shapes=[
            pltpu.VMEM((2, visits, height, width), F32),
            pltpu.VMEM((terms, pieces + 2, height, PC), F32),
            pltpu.VMEM((pieces, height, PC), F32),
            pltpu.VMEM((2, n, height, PC), F32),
            pltpu.VMEM((2, n, height, PC), F32),
            pltpu.SemaphoreType.DMA((2, visits)),
            pltpu.SemaphoreType.DMA((2, visits)),
            pltpu.SemaphoreType.DMA((2, n)),
            pltpu.SemaphoreType.DMA((2, n)),
        ],
        compiler_params=pltpu.CompilerParams(
            collective_id=0, has_side_effects=True, vmem_limit_bytes=48 * 1024 * 1024
        ),
    )(image, inv_var, rows_op, cols_op, edge_op, hot)


def solution(mesh):
    in_specs = (
        P(None, ("groups", "tile"), None),
        P(None, ("groups", "tile"), None),
        P("groups", None),
        P("groups"),
        P("groups", None, None),
        P("groups", None, None),
        P(("groups", "tile"), None),
    )
    out_specs = (P(None, ("groups", "tile"), None), P(("groups", "tile"), None, None))
    return jax.shard_map(
        on_device, mesh=mesh, in_specs=in_specs, out_specs=out_specs, check_vma=False
    )
```

```python
import functools

import jax
import jax.numpy as jnp
from jax import lax
from jax.experimental import pallas as pl
from jax.experimental.pallas import tpu as pltpu
from jax.sharding import PartitionSpec as P

PC = 128
LEAD = 20
BF = jnp.bfloat16
F32 = jnp.float32


def lanczos(values):
    return jnp.where(jnp.abs(values) < 3.0, jnp.sinc(values) * jnp.sinc(values / 3.0), 0.0)


def tap_weights(fraction):
    places = jnp.arange(-3, 4).astype(F32)
    weights = lanczos(places[None, :] + fraction[:, None])
    return weights / jnp.sum(weights, axis=1, keepdims=True)


def two_terms(x):
    high = x.astype(BF)
    return high, (x - high.astype(F32)).astype(BF)


def rounded_terms(x):
    high = lax.reduce_precision(x, exponent_bits=8, mantissa_bits=7)
    return high.astype(BF), (x - high).astype(BF)


def pick(weights, index):
    total = 0.0
    for t in range(weights.shape[1]):
        w = weights[:, t].reshape((-1,) + (1,) * (index.ndim - 1))
        total = total + jnp.where(index == t, w, 0.0)
    return total


def row_operator(row_tap, psf_rows, height, me, n):
    visits, terms, _ = psf_rows.shape
    i = jnp.arange(height, dtype=jnp.int32)[:, None, None]
    m = jnp.arange(height + 40, dtype=jnp.int32)[None, :, None]
    select = (i - m + 40 == jnp.arange(41, dtype=jnp.int32)[None, None, :]).astype(F32)
    band = jnp.einsum("vka,ima->vkim", psf_rows, select, precision=lax.Precision.HIGHEST)
    mi = jnp.arange(height + 40, dtype=jnp.int32)[:, None]
    ri = jnp.arange(3 * height, dtype=jnp.int32)[None, :]
    taps = pick(row_tap, (mi - ri + height - LEAD + 3)[None])
    row = me * height + mi - LEAD
    taps = jnp.where((row >= 0) & (row < n * height), taps, 0.0)
    full = jnp.einsum("vkim,vmr->vkir", band, taps, precision=lax.Precision.HIGHEST)
    full = full.reshape(visits, terms * height, 3 * height)
    high, low = rounded_terms(full)
    stacked = jnp.concatenate([high, high, low], axis=2)
    rows = -(-stacked.shape[1] // 16) * 16
    depth = -(-stacked.shape[2] // 256) * 256
    return jnp.pad(
        stacked, ((0, 0), (0, rows - stacked.shape[1]), (0, depth - stacked.shape[2]))
    )


def edge_operator(col_tap, col_offset, psf_cols):
    visits, terms, _ = psf_cols.shape
    m = jnp.arange(PC, dtype=jnp.int32)[:, None]
    j = jnp.arange(LEAD, dtype=jnp.int32)[None, :]
    place = jnp.stack([j - LEAD - m, PC + j - m])[None] - col_offset[:, None, None, None]
    taps = pick(col_tap, place + 3)
    jj = jnp.arange(LEAD, dtype=jnp.int32)[:, None]
    o = jnp.arange(PC, dtype=jnp.int32)[None, :]
    index = jnp.stack([o - jj + 40, o - PC - jj + 20])
    select = (index[..., None] == jnp.arange(41, dtype=jnp.int32)).astype(F32)
    psf = jnp.einsum("vkb,ejob->vkejo", psf_cols, select, precision=lax.Precision.HIGHEST)
    full = jnp.einsum("vemj,vkejo->vekmo", taps, psf, precision=lax.Precision.HIGHEST)
    high, low = rounded_terms(full.reshape(visits, 2, terms * PC, PC))
    return jnp.concatenate([high, low], axis=3)


def band_kernel(terms, c_ref, out_ref):
    for k in range(terms):
        row = jnp.broadcast_to(c_ref[0, k : k + 1, :], (PC, 2 * PC))
        turned = pltpu.roll(row, 0, 1, stride=1, stride_axis=0)
        m = lax.broadcasted_iota(jnp.int32, (PC, PC), 0)
        o = lax.broadcasted_iota(jnp.int32, (PC, PC), 1)
        far = turned[:, PC:]
        for d, part in enumerate(
            [jnp.where(o < m, far, 0.0), turned[:, :PC], jnp.where(o > m, far, 0.0)]
        ):
            high = part.astype(BF)
            low = (part - high.astype(F32)).astype(BF)
            start = (3 * k + d) * PC
            out_ref[0, start : start + PC, :PC] = high
            out_ref[0, start : start + PC, PC:] = low


def col_operator(col_tap, col_offset, psf_cols):
    visits, terms, _ = psf_cols.shape
    b = jnp.arange(41, dtype=jnp.int32)[:, None]
    lane = jnp.arange(2 * PC, dtype=jnp.int32)[None, :]
    signed = jnp.where(lane < PC, lane, lane - 2 * PC)
    spread = pick(col_tap, (signed - b + LEAD + 3)[None] - col_offset[:, None, None])
    line = jnp.einsum("vkb,vbl->vkl", psf_cols, spread, precision=lax.Precision.HIGHEST)
    return pl.pallas_call(
        functools.partial(band_kernel, terms),
        grid=(visits,),
        in_specs=[pl.BlockSpec((1, terms, 2 * PC), lambda v: (v, 0, 0))],
        out_specs=pl.BlockSpec((1, terms * 3 * PC, 2 * PC), lambda v: (v, 0, 0)),
        out_shape=jax.ShapeDtypeStruct((visits, terms * 3 * PC, 2 * PC), BF),
    )(line)


def split_dot(x, w_ref):
    high, low = two_terms(x)
    wide = jnp.dot(high, w_ref[...], preferred_element_type=F32)
    narrow = jnp.dot(low, w_ref[:, :PC], preferred_element_type=F32)
    return wide[:, :PC] + wide[:, PC:] + narrow


def main_kernel(
    n, terms, image, before, after, inv_var, rows_op, cols_op, edge_op, hot, out_m, out_c,
    halo, lines, block, sums, got, halo_send, halo_recv, sum_send, sum_recv,
):
    visits, height, width = image.shape
    pieces = width // PC
    early = before.shape[0]
    me = lax.axis_index("tile")

    barrier = pltpu.get_barrier_semaphore()

    def greet(d, carry):
        pl.semaphore_signal(
            barrier, inc=1, device_id={"tile": lax.rem(me + d, n)},
            device_id_type=pl.DeviceIdType.MESH,
        )
        return carry

    lax.fori_loop(1, n, greet, 0)
    pl.semaphore_wait(barrier, n - 1)

    def halo_copy(v, side):
        other = me + 1 if side == 0 else me - 1
        return pltpu.make_async_remote_copy(
            src_ref=image.at[v], dst_ref=halo.at[side, v - early],
            send_sem=halo_send.at[side, v - early], recv_sem=halo_recv.at[side, v - early],
            device_id={"tile": other}, device_id_type=pl.DeviceIdType.MESH,
        )

    for v in range(early, visits):
        @pl.when(me < n - 1)
        def _():
            halo_copy(v, 0).start()

        @pl.when(me > 0)
        def _():
            halo_copy(v, 1).start()

    @pl.when(me == 0)
    def _():
        halo[0] = jnp.zeros_like(halo[0])

    @pl.when(me == n - 1)
    def _():
        halo[1] = jnp.zeros_like(halo[1])

    def add_up(v, which, first):
        def owner(p, carry):
            total = jnp.zeros((height, PC), F32) if first else sums[which, p]
            for c in range(pieces):
                total = total + hot[(v * pieces + c) * n + p] * block[c]
            sums[which, p] = total
            return carry

        lax.fori_loop(0, n, owner, 0)

    def sum_copy(which, d):
        return pltpu.make_async_remote_copy(
            src_ref=sums.at[which, lax.rem(me + d, n)], dst_ref=got.at[which, me],
            send_sem=sum_send.at[which, d], recv_sem=sum_recv.at[which, me],
            device_id={"tile": lax.rem(me + d, n)}, device_id_type=pl.DeviceIdType.MESH,
        )

    def send_sums(which):
        def one(d, carry):
            sum_copy(which, d).start()
            return carry

        lax.fori_loop(1, n, one, 0)

    for v in range(visits):
        for c in range(pieces):
            block[c] = inv_var[v, :, c * PC : (c + 1) * PC]
        add_up(v, 1, v == 0)
    send_sums(1)

    for k in range(terms):
        lines[k, 0] = jnp.zeros((height, PC), F32)
        lines[k, pieces + 1] = jnp.zeros((height, PC), F32)

    depth = rows_op.shape[2]
    step = 4
    for v in range(visits):
        if v < early:
            above, below = before.at[v], after.at[v]
        else:
            above, below = halo.at[0, v - early], halo.at[1, v - early]

            @pl.when(me > 0)
            def _():
                pltpu.make_async_copy(image.at[v], above, halo_recv.at[0, v - early]).wait()

            @pl.when(me < n - 1)
            def _():
                pltpu.make_async_copy(image.at[v], below, halo_recv.at[1, v - early]).wait()

        def rows_stage(q, carry, above=above, below=below, v=v):
            cols = pl.ds(pl.multiple_of(q * (step * PC), step * PC), step * PC)
            x = jnp.concatenate([above[:, cols], image[v, :, cols], below[:, cols]], 0)
            high = x.astype(BF).astype(F32)
            rest = jnp.zeros((depth - 9 * height, step * PC), F32)
            stacked = jnp.concatenate([high, x - high, high, rest], 0).astype(BF)
            y = jnp.dot(rows_op[v], stacked, preferred_element_type=F32)
            for k in range(terms):
                for s in range(step):
                    lines[k, q * step + s + 1] = y[
                        k * height : (k + 1) * height, s * PC : (s + 1) * PC
                    ]
            return carry

        lax.fori_loop(0, pieces // step, rows_stage, 0)

        half = pieces // 2

        def cols_stage(q, carry):
            parts = [
                lines[k, pl.ds(q * half + d, half)].reshape(half * height, PC)
                for k in range(terms)
                for d in range(3)
            ]
            res = split_dot(jnp.concatenate(parts, 1), cols_op.at[v])
            block[pl.ds(q * half, half)] = res.reshape(half, height, PC)
            return carry

        lax.fori_loop(0, 2, cols_stage, 0)
        for e, c in ((0, 0), (1, pieces - 1)):
            x = jnp.concatenate([lines[k, c + 1] for k in range(terms)], 1)
            block[c] = block[c] - split_dot(x, edge_op.at[v, e])
        for c in range(pieces):
            cols = slice(c * PC, (c + 1) * PC)
            value = block[c]
            out_m[v, :, cols] = value.astype(BF)
            block[c] = value * inv_var[v, :, cols]
        add_up(v, 0, v == 0)
    send_sums(0)

    totals = []
    for which in (1, 0):
        def one(d, total):
            source = lax.rem(me + n - d, n)
            pltpu.make_async_copy(
                sums.at[which, 0], got.at[which, source], sum_recv.at[which, source]
            ).wait()
            return total + got[which, source]

        totals.append(lax.fori_loop(1, n, one, sums[which, me]))
    out_c[0] = totals[1] / jnp.maximum(totals[0], 1.0)

    for which in (0, 1):
        def done(d, carry):
            sum_copy(which, d).wait_send()
            return carry

        lax.fori_loop(1, n, done, 0)
    for v in range(early, visits):
        @pl.when(me < n - 1)
        def _():
            halo_copy(v, 0).wait_send()

        @pl.when(me > 0)
        def _():
            halo_copy(v, 1).wait_send()


def on_device(image, inv_var, shift, col_offset, psf_rows, psf_cols, placement):
    visits, height, width = image.shape
    n = lax.axis_size("tile")
    me = lax.axis_index("tile")
    terms = psf_rows.shape[1]
    pieces = width // PC
    early = visits // 2
    up = [(i, i + 1) for i in range(n - 1)]
    before = lax.ppermute(image[:early], "tile", up)
    after = lax.ppermute(image[:early], "tile", [(j, i) for i, j in up])
    row_tap = tap_weights(shift[:, 0])
    col_tap = tap_weights(shift[:, 1])
    rows_op = row_operator(row_tap, psf_rows, height, me, n)
    cols_op = col_operator(col_tap, col_offset, psf_cols)
    edge_op = edge_operator(col_tap, col_offset, psf_cols)
    hot = (placement == jnp.arange(n, dtype=jnp.int32)[None, :]).astype(F32).reshape(-1)
    vmem = pl.BlockSpec(memory_space=pltpu.VMEM)
    return pl.pallas_call(
        functools.partial(main_kernel, n, terms),
        out_shape=(
            jax.ShapeDtypeStruct((visits, height, width), BF),
            jax.ShapeDtypeStruct((1, height, PC), F32),
        ),
        in_specs=[vmem] * 7 + [pl.BlockSpec(memory_space=pltpu.SMEM)],
        out_specs=(vmem, vmem),
        scratch_shapes=[
            pltpu.VMEM((2, visits - early, height, width), F32),
            pltpu.VMEM((terms, pieces + 2, height, PC), F32),
            pltpu.VMEM((pieces, height, PC), F32),
            pltpu.VMEM((2, n, height, PC), F32),
            pltpu.VMEM((2, n, height, PC), F32),
            pltpu.SemaphoreType.DMA((2, visits - early)),
            pltpu.SemaphoreType.DMA((2, visits - early)),
            pltpu.SemaphoreType.DMA((2, n)),
            pltpu.SemaphoreType.DMA((2, n)),
        ],
        compiler_params=pltpu.CompilerParams(
            collective_id=0, has_side_effects=True, vmem_limit_bytes=48 * 1024 * 1024
        ),
    )(image, before, after, inv_var, rows_op, cols_op, edge_op, hot)


def solution(mesh):
    in_specs = (
        P(None, ("groups", "tile"), None),
        P(None, ("groups", "tile"), None),
        P("groups", None),
        P("groups"),
        P("groups", None, None),
        P("groups", None, None),
        P(("groups", "tile"), None),
    )
    out_specs = (P(None, ("groups", "tile"), None), P(("groups", "tile"), None, None))
    return jax.shard_map(
        on_device, mesh=mesh, in_specs=in_specs, out_specs=out_specs, check_vma=False
    )
```

```python
import functools

import jax
import jax.numpy as jnp
from jax import lax
from jax.experimental import pallas as pl
from jax.experimental.pallas import tpu as pltpu
from jax.sharding import PartitionSpec as P

PC = 128
LEAD = 20
BF = jnp.bfloat16
F32 = jnp.float32


def lanczos(values):
    return jnp.where(jnp.abs(values) < 3.0, jnp.sinc(values) * jnp.sinc(values / 3.0), 0.0)


def tap_weights(fraction):
    places = jnp.arange(-3, 4).astype(F32)
    weights = lanczos(places[None, :] + fraction[:, None])
    return weights / jnp.sum(weights, axis=1, keepdims=True)


def two_terms(x):
    high = x.astype(BF)
    return high, (x - high.astype(F32)).astype(BF)


def rounded_terms(x):
    high = lax.reduce_precision(x, exponent_bits=8, mantissa_bits=7)
    return high.astype(BF), (x - high).astype(BF)


def pick(weights, index):
    total = 0.0
    for t in range(weights.shape[1]):
        w = weights[:, t].reshape((-1,) + (1,) * (index.ndim - 1))
        total = total + jnp.where(index == t, w, 0.0)
    return total


def row_operator(row_tap, psf_rows, height, me, n):
    visits, terms, _ = psf_rows.shape
    i = jnp.arange(height, dtype=jnp.int32)[:, None, None]
    m = jnp.arange(height + 40, dtype=jnp.int32)[None, :, None]
    select = (i - m + 40 == jnp.arange(41, dtype=jnp.int32)[None, None, :]).astype(F32)
    band = jnp.einsum("vka,ima->vkim", psf_rows, select, precision=lax.Precision.HIGHEST)
    mi = jnp.arange(height + 40, dtype=jnp.int32)[:, None]
    ri = jnp.arange(3 * height, dtype=jnp.int32)[None, :]
    taps = pick(row_tap, (mi - ri + height - LEAD + 3)[None])
    row = me * height + mi - LEAD
    taps = jnp.where((row >= 0) & (row < n * height), taps, 0.0)
    full = jnp.einsum("vkim,vmr->vkir", band, taps, precision=lax.Precision.HIGHEST)
    full = full.reshape(visits, terms * height, 3 * height)
    high, low = rounded_terms(full)
    stacked = jnp.concatenate([high, high, low], axis=2)
    rows = -(-stacked.shape[1] // 16) * 16
    depth = -(-stacked.shape[2] // 256) * 256
    return jnp.pad(
        stacked, ((0, 0), (0, rows - stacked.shape[1]), (0, depth - stacked.shape[2]))
    )


def edge_operator(col_tap, col_offset, psf_cols):
    visits, terms, _ = psf_cols.shape
    m = jnp.arange(PC, dtype=jnp.int32)[:, None]
    j = jnp.arange(LEAD, dtype=jnp.int32)[None, :]
    place = jnp.stack([j - LEAD - m, PC + j - m])[None] - col_offset[:, None, None, None]
    taps = pick(col_tap, place + 3)
    jj = jnp.arange(LEAD, dtype=jnp.int32)[:, None]
    o = jnp.arange(PC, dtype=jnp.int32)[None, :]
    index = jnp.stack([o - jj + 40, o - PC - jj + 20])
    select = (index[..., None] == jnp.arange(41, dtype=jnp.int32)).astype(F32)
    psf = jnp.einsum("vkb,ejob->vkejo", psf_cols, select, precision=lax.Precision.HIGHEST)
    full = jnp.einsum("vemj,vkejo->vekmo", taps, psf, precision=lax.Precision.HIGHEST)
    high, low = rounded_terms(full.reshape(visits, 2, terms * PC, PC))
    return jnp.concatenate([high, low], axis=3)


def band_kernel(terms, c_ref, out_ref):
    for k in range(terms):
        row = jnp.broadcast_to(c_ref[0, k : k + 1, :], (PC, 2 * PC))
        turned = pltpu.roll(row, 0, 1, stride=1, stride_axis=0)
        m = lax.broadcasted_iota(jnp.int32, (PC, PC), 0)
        o = lax.broadcasted_iota(jnp.int32, (PC, PC), 1)
        far = turned[:, PC:]
        for d, part in enumerate(
            [jnp.where(o < m, far, 0.0), turned[:, :PC], jnp.where(o > m, far, 0.0)]
        ):
            high = part.astype(BF)
            low = (part - high.astype(F32)).astype(BF)
            start = (3 * k + d) * PC
            out_ref[0, start : start + PC, :PC] = high
            out_ref[0, start : start + PC, PC:] = low


def col_operator(col_tap, col_offset, psf_cols):
    visits, terms, _ = psf_cols.shape
    b = jnp.arange(41, dtype=jnp.int32)[:, None]
    lane = jnp.arange(2 * PC, dtype=jnp.int32)[None, :]
    signed = jnp.where(lane < PC, lane, lane - 2 * PC)
    spread = pick(col_tap, (signed - b + LEAD + 3)[None] - col_offset[:, None, None])
    line = jnp.einsum("vkb,vbl->vkl", psf_cols, spread, precision=lax.Precision.HIGHEST)
    return pl.pallas_call(
        functools.partial(band_kernel, terms),
        grid=(visits,),
        in_specs=[pl.BlockSpec((1, terms, 2 * PC), lambda v: (v, 0, 0))],
        out_specs=pl.BlockSpec((1, terms * 3 * PC, 2 * PC), lambda v: (v, 0, 0)),
        out_shape=jax.ShapeDtypeStruct((visits, terms * 3 * PC, 2 * PC), BF),
    )(line)


def split_dot(x, w_ref):
    high, low = two_terms(x)
    wide = jnp.dot(high, w_ref[...], preferred_element_type=F32)
    narrow = jnp.dot(low, w_ref[:, :PC], preferred_element_type=F32)
    return wide[:, :PC] + wide[:, PC:] + narrow


def main_kernel(
    n, terms, image, before, after, inv_var, rows_op, cols_op, edge_op, hot, out_m, out_c,
    halo, lines, block, sums, got, halo_send, halo_recv, sum_send, sum_recv,
):
    visits, height, width = image.shape
    pieces = width // PC
    early = before.shape[0]
    me = lax.axis_index("tile")

    barrier = pltpu.get_barrier_semaphore()

    def greet(d, carry):
        pl.semaphore_signal(
            barrier, inc=1, device_id={"tile": lax.rem(me + d, n)},
            device_id_type=pl.DeviceIdType.MESH,
        )
        return carry

    lax.fori_loop(1, n, greet, 0)
    pl.semaphore_wait(barrier, n - 1)

    def halo_copy(v, side):
        other = me + 1 if side == 0 else me - 1
        return pltpu.make_async_remote_copy(
            src_ref=image.at[v], dst_ref=halo.at[side, v - early],
            send_sem=halo_send.at[side, v - early], recv_sem=halo_recv.at[side, v - early],
            device_id={"tile": other}, device_id_type=pl.DeviceIdType.MESH,
        )

    for v in range(early, visits):
        @pl.when(me < n - 1)
        def _():
            halo_copy(v, 0).start()

        @pl.when(me > 0)
        def _():
            halo_copy(v, 1).start()

    @pl.when(me == 0)
    def _():
        halo[0] = jnp.zeros_like(halo[0])

    @pl.when(me == n - 1)
    def _():
        halo[1] = jnp.zeros_like(halo[1])

    def add_up(v, which, first):
        group = 8 if n % 8 == 0 else 1

        def owners(q, carry):
            p = q * group
            totals = [
                jnp.zeros((height, PC), F32) if first else sums[which, p + g]
                for g in range(group)
            ]
            for c in range(pieces):
                piece = block[c]
                for g in range(group):
                    totals[g] = totals[g] + hot[(v * pieces + c) * n + p + g] * piece
            for g in range(group):
                sums[which, p + g] = totals[g]
            return carry

        lax.fori_loop(0, n // group, owners, 0)

    def sum_copy(which, d):
        return pltpu.make_async_remote_copy(
            src_ref=sums.at[which, lax.rem(me + d, n)], dst_ref=got.at[which, me],
            send_sem=sum_send.at[which, d], recv_sem=sum_recv.at[which, me],
            device_id={"tile": lax.rem(me + d, n)}, device_id_type=pl.DeviceIdType.MESH,
        )

    def send_sums(which):
        def one(d, carry):
            sum_copy(which, d).start()
            return carry

        lax.fori_loop(1, n, one, 0)

    for v in range(visits):
        for c in range(pieces):
            block[c] = inv_var[v, :, c * PC : (c + 1) * PC]
        add_up(v, 1, v == 0)
    send_sums(1)

    for k in range(terms):
        lines[k, 0] = jnp.zeros((height, PC), F32)
        lines[k, pieces + 1] = jnp.zeros((height, PC), F32)

    depth = rows_op.shape[2]
    step = 4
    for v in range(visits):
        if v < early:
            above, below = before.at[v], after.at[v]
        else:
            above, below = halo.at[0, v - early], halo.at[1, v - early]

            @pl.when(me > 0)
            def _():
                pltpu.make_async_copy(image.at[v], above, halo_recv.at[0, v - early]).wait()

            @pl.when(me < n - 1)
            def _():
                pltpu.make_async_copy(image.at[v], below, halo_recv.at[1, v - early]).wait()

        def rows_stage(q, carry, above=above, below=below, v=v):
            cols = pl.ds(pl.multiple_of(q * (step * PC), step * PC), step * PC)
            x = jnp.concatenate([above[:, cols], image[v, :, cols], below[:, cols]], 0)
            high = x.astype(BF).astype(F32)
            rest = jnp.zeros((depth - 9 * height, step * PC), F32)
            stacked = jnp.concatenate([high, x - high, high, rest], 0).astype(BF)
            y = jnp.dot(rows_op[v], stacked, preferred_element_type=F32)
            for k in range(terms):
                for s in range(step):
                    lines[k, q * step + s + 1] = y[
                        k * height : (k + 1) * height, s * PC : (s + 1) * PC
                    ]
            return carry

        lax.fori_loop(0, pieces // step, rows_stage, 0)

        half = pieces // 2

        def cols_stage(q, carry):
            parts = [
                lines[k, pl.ds(q * half + d, half)].reshape(half * height, PC)
                for k in range(terms)
                for d in range(3)
            ]
            res = split_dot(jnp.concatenate(parts, 1), cols_op.at[v])
            block[pl.ds(q * half, half)] = res.reshape(half, height, PC)
            return carry

        lax.fori_loop(0, 2, cols_stage, 0)
        for e, c in ((0, 0), (1, pieces - 1)):
            x = jnp.concatenate([lines[k, c + 1] for k in range(terms)], 1)
            block[c] = block[c] - split_dot(x, edge_op.at[v, e])
        for c in range(pieces):
            cols = slice(c * PC, (c + 1) * PC)
            value = block[c]
            out_m[v, :, cols] = value.astype(BF)
            block[c] = value * inv_var[v, :, cols]
        add_up(v, 0, v == 0)
    send_sums(0)

    totals = []
    for which in (1, 0):
        def one(d, total):
            source = lax.rem(me + n - d, n)
            pltpu.make_async_copy(
                sums.at[which, 0], got.at[which, source], sum_recv.at[which, source]
            ).wait()
            return total + got[which, source]

        totals.append(lax.fori_loop(1, n, one, sums[which, me]))
    out_c[0] = totals[1] / jnp.maximum(totals[0], 1.0)

    for which in (0, 1):
        def done(d, carry):
            sum_copy(which, d).wait_send()
            return carry

        lax.fori_loop(1, n, done, 0)
    for v in range(early, visits):
        @pl.when(me < n - 1)
        def _():
            halo_copy(v, 0).wait_send()

        @pl.when(me > 0)
        def _():
            halo_copy(v, 1).wait_send()


def on_device(image, inv_var, shift, col_offset, psf_rows, psf_cols, placement):
    visits, height, width = image.shape
    n = lax.axis_size("tile")
    me = lax.axis_index("tile")
    terms = psf_rows.shape[1]
    pieces = width // PC
    early = visits // 2
    up = [(i, i + 1) for i in range(n - 1)]
    before = lax.ppermute(image[:early], "tile", up)
    after = lax.ppermute(image[:early], "tile", [(j, i) for i, j in up])
    row_tap = tap_weights(shift[:, 0])
    col_tap = tap_weights(shift[:, 1])
    rows_op = row_operator(row_tap, psf_rows, height, me, n)
    cols_op = col_operator(col_tap, col_offset, psf_cols)
    edge_op = edge_operator(col_tap, col_offset, psf_cols)
    hot = (placement == jnp.arange(n, dtype=jnp.int32)[None, :]).astype(F32).reshape(-1)
    vmem = pl.BlockSpec(memory_space=pltpu.VMEM)
    return pl.pallas_call(
        functools.partial(main_kernel, n, terms),
        out_shape=(
            jax.ShapeDtypeStruct((visits, height, width), BF),
            jax.ShapeDtypeStruct((1, height, PC), F32),
        ),
        in_specs=[vmem] * 7 + [pl.BlockSpec(memory_space=pltpu.SMEM)],
        out_specs=(vmem, vmem),
        scratch_shapes=[
            pltpu.VMEM((2, visits - early, height, width), F32),
            pltpu.VMEM((terms, pieces + 2, height, PC), F32),
            pltpu.VMEM((pieces, height, PC), F32),
            pltpu.VMEM((2, n, height, PC), F32),
            pltpu.VMEM((2, n, height, PC), F32),
            pltpu.SemaphoreType.DMA((2, visits - early)),
            pltpu.SemaphoreType.DMA((2, visits - early)),
            pltpu.SemaphoreType.DMA((2, n)),
            pltpu.SemaphoreType.DMA((2, n)),
        ],
        compiler_params=pltpu.CompilerParams(
            collective_id=0, has_side_effects=True, vmem_limit_bytes=48 * 1024 * 1024
        ),
    )(image, before, after, inv_var, rows_op, cols_op, edge_op, hot)


def solution(mesh):
    in_specs = (
        P(None, ("groups", "tile"), None),
        P(None, ("groups", "tile"), None),
        P("groups", None),
        P("groups"),
        P("groups", None, None),
        P("groups", None, None),
        P(("groups", "tile"), None),
    )
    out_specs = (P(None, ("groups", "tile"), None), P(("groups", "tile"), None, None))
    return jax.shard_map(
        on_device, mesh=mesh, in_specs=in_specs, out_specs=out_specs, check_vma=False
    )
```

```python
import functools

import jax
import jax.numpy as jnp
from jax import lax
from jax.experimental import pallas as pl
from jax.experimental.pallas import tpu as pltpu
from jax.sharding import PartitionSpec as P

PC = 128
LEAD = 20
BF = jnp.bfloat16
F32 = jnp.float32


def lanczos(values):
    return jnp.where(jnp.abs(values) < 3.0, jnp.sinc(values) * jnp.sinc(values / 3.0), 0.0)


def tap_weights(fraction):
    places = jnp.arange(-3, 4).astype(F32)
    weights = lanczos(places[None, :] + fraction[:, None])
    return weights / jnp.sum(weights, axis=1, keepdims=True)


def two_terms(x):
    high = x.astype(BF)
    return high, (x - high.astype(F32)).astype(BF)


def rounded_terms(x):
    high = lax.reduce_precision(x, exponent_bits=8, mantissa_bits=7)
    return high.astype(BF), (x - high).astype(BF)


def pick(weights, index):
    total = 0.0
    for t in range(weights.shape[1]):
        w = weights[:, t].reshape((-1,) + (1,) * (index.ndim - 1))
        total = total + jnp.where(index == t, w, 0.0)
    return total


def row_operator(row_tap, psf_rows, height, me, n):
    visits, terms, _ = psf_rows.shape
    i = jnp.arange(height, dtype=jnp.int32)[:, None, None]
    m = jnp.arange(height + 40, dtype=jnp.int32)[None, :, None]
    select = (i - m + 40 == jnp.arange(41, dtype=jnp.int32)[None, None, :]).astype(F32)
    band = jnp.einsum("vka,ima->vkim", psf_rows, select, precision=lax.Precision.HIGHEST)
    mi = jnp.arange(height + 40, dtype=jnp.int32)[:, None]
    ri = jnp.arange(3 * height, dtype=jnp.int32)[None, :]
    taps = pick(row_tap, (mi - ri + height - LEAD + 3)[None])
    row = me * height + mi - LEAD
    taps = jnp.where((row >= 0) & (row < n * height), taps, 0.0)
    full = jnp.einsum("vkim,vmr->vkir", band, taps, precision=lax.Precision.HIGHEST)
    full = full.reshape(visits, terms * height, 3 * height)
    high, low = rounded_terms(full)
    stacked = jnp.concatenate([high, high, low], axis=2)
    rows = -(-stacked.shape[1] // 16) * 16
    depth = -(-stacked.shape[2] // 256) * 256
    return jnp.pad(
        stacked, ((0, 0), (0, rows - stacked.shape[1]), (0, depth - stacked.shape[2]))
    )


def edge_operator(col_tap, col_offset, psf_cols):
    visits, terms, _ = psf_cols.shape
    m = jnp.arange(PC, dtype=jnp.int32)[:, None]
    j = jnp.arange(LEAD, dtype=jnp.int32)[None, :]
    place = jnp.stack([j - LEAD - m, PC + j - m])[None] - col_offset[:, None, None, None]
    taps = pick(col_tap, place + 3)
    jj = jnp.arange(LEAD, dtype=jnp.int32)[:, None]
    o = jnp.arange(PC, dtype=jnp.int32)[None, :]
    index = jnp.stack([o - jj + 40, o - PC - jj + 20])
    select = (index[..., None] == jnp.arange(41, dtype=jnp.int32)).astype(F32)
    psf = jnp.einsum("vkb,ejob->vkejo", psf_cols, select, precision=lax.Precision.HIGHEST)
    full = jnp.einsum("vemj,vkejo->vekmo", taps, psf, precision=lax.Precision.HIGHEST)
    high, low = rounded_terms(full.reshape(visits, 2, terms * PC, PC))
    return jnp.concatenate([high, low], axis=3)


def band_kernel(terms, c_ref, out_ref):
    for k in range(terms):
        row = jnp.broadcast_to(c_ref[0, k : k + 1, :], (PC, 2 * PC))
        turned = pltpu.roll(row, 0, 1, stride=1, stride_axis=0)
        m = lax.broadcasted_iota(jnp.int32, (PC, PC), 0)
        o = lax.broadcasted_iota(jnp.int32, (PC, PC), 1)
        far = turned[:, PC:]
        for d, part in enumerate(
            [jnp.where(o < m, far, 0.0), turned[:, :PC], jnp.where(o > m, far, 0.0)]
        ):
            high = part.astype(BF)
            low = (part - high.astype(F32)).astype(BF)
            start = (3 * k + d) * PC
            out_ref[0, start : start + PC, :PC] = high
            out_ref[0, start : start + PC, PC:] = low


def col_operator(col_tap, col_offset, psf_cols):
    visits, terms, _ = psf_cols.shape
    b = jnp.arange(41, dtype=jnp.int32)[:, None]
    lane = jnp.arange(2 * PC, dtype=jnp.int32)[None, :]
    signed = jnp.where(lane < PC, lane, lane - 2 * PC)
    spread = pick(col_tap, (signed - b + LEAD + 3)[None] - col_offset[:, None, None])
    line = jnp.einsum("vkb,vbl->vkl", psf_cols, spread, precision=lax.Precision.HIGHEST)
    return pl.pallas_call(
        functools.partial(band_kernel, terms),
        grid=(visits,),
        in_specs=[pl.BlockSpec((1, terms, 2 * PC), lambda v: (v, 0, 0))],
        out_specs=pl.BlockSpec((1, terms * 3 * PC, 2 * PC), lambda v: (v, 0, 0)),
        out_shape=jax.ShapeDtypeStruct((visits, terms * 3 * PC, 2 * PC), BF),
    )(line)


def split_dot(x, w_ref):
    high, low = two_terms(x)
    wide = jnp.dot(high, w_ref[...], preferred_element_type=F32)
    narrow = jnp.dot(low, w_ref[:, :PC], preferred_element_type=F32)
    return wide[:, :PC] + wide[:, PC:] + narrow


def main_kernel(
    n, terms, image, before, after, inv_var, rows_op, cols_op, edge_op, hot, out_m, out_c,
    halo, lines, block, sums, got, halo_send, halo_recv, sum_send, sum_recv,
):
    visits, height, width = image.shape
    pieces = width // PC
    early = before.shape[0]
    me = lax.axis_index("tile")

    barrier = pltpu.get_barrier_semaphore()

    def greet(d, carry):
        pl.semaphore_signal(
            barrier, inc=1, device_id={"tile": lax.rem(me + d, n)},
            device_id_type=pl.DeviceIdType.MESH,
        )
        return carry

    lax.fori_loop(1, n, greet, 0)
    pl.semaphore_wait(barrier, n - 1)

    def halo_copy(v, side):
        other = me + 1 if side == 0 else me - 1
        return pltpu.make_async_remote_copy(
            src_ref=image.at[v], dst_ref=halo.at[side, v - early],
            send_sem=halo_send.at[side, v - early], recv_sem=halo_recv.at[side, v - early],
            device_id={"tile": other}, device_id_type=pl.DeviceIdType.MESH,
        )

    for v in range(early, visits):
        @pl.when(me < n - 1)
        def _():
            halo_copy(v, 0).start()

        @pl.when(me > 0)
        def _():
            halo_copy(v, 1).start()

    @pl.when(me == 0)
    def _():
        halo[0] = jnp.zeros_like(halo[0])

    @pl.when(me == n - 1)
    def _():
        halo[1] = jnp.zeros_like(halo[1])

    def add_up(v, which, first):
        def owner(p, carry):
            total = jnp.zeros((height, PC), F32) if first else sums[which, p]
            for c in range(pieces):
                total = total + hot[(v * pieces + c) * n + p] * block[c]
            sums[which, p] = total
            return carry

        lax.fori_loop(0, n, owner, 0)

    def sum_copy(which, d):
        return pltpu.make_async_remote_copy(
            src_ref=sums.at[which, lax.rem(me + d, n)], dst_ref=got.at[which, me],
            send_sem=sum_send.at[which, d], recv_sem=sum_recv.at[which, me],
            device_id={"tile": lax.rem(me + d, n)}, device_id_type=pl.DeviceIdType.MESH,
        )

    def send_sums(which):
        def one(d, carry):
            sum_copy(which, d).start()
            return carry

        lax.fori_loop(1, n, one, 0)

    for v in range(visits):
        for c in range(pieces):
            block[c] = inv_var[v, :, c * PC : (c + 1) * PC]
        add_up(v, 1, v == 0)
    send_sums(1)

    for k in range(terms):
        lines[k, 0] = jnp.zeros((height, PC), F32)
        lines[k, pieces + 1] = jnp.zeros((height, PC), F32)

    depth = rows_op.shape[2]
    step = 4
    for v in range(visits):
        if v < early:
            above, below = before.at[v], after.at[v]
        else:
            above, below = halo.at[0, v - early], halo.at[1, v - early]

            @pl.when(me > 0)
            def _():
                pltpu.make_async_copy(image.at[v], above, halo_recv.at[0, v - early]).wait()

            @pl.when(me < n - 1)
            def _():
                pltpu.make_async_copy(image.at[v], below, halo_recv.at[1, v - early]).wait()

        def rows_stage(q, carry, above=above, below=below, v=v):
            cols = pl.ds(pl.multiple_of(q * (step * PC), step * PC), step * PC)
            x = jnp.concatenate([above[:, cols], image[v, :, cols], below[:, cols]], 0)
            high = x.astype(BF).astype(F32)
            rest = jnp.zeros((depth - 9 * height, step * PC), F32)
            stacked = jnp.concatenate([high, x - high, high, rest], 0).astype(BF)
            y = jnp.dot(rows_op[v], stacked, preferred_element_type=F32)
            for k in range(terms):
                for s in range(step):
                    lines[k, q * step + s + 1] = y[
                        k * height : (k + 1) * height, s * PC : (s + 1) * PC
                    ]
            return carry

        lax.fori_loop(0, pieces // step, rows_stage, 0)

        half = pieces // 2

        def cols_stage(q, carry):
            parts = [
                lines[k, pl.ds(q * half + d, half)].reshape(half * height, PC)
                for k in range(terms)
                for d in range(3)
            ]
            res = split_dot(jnp.concatenate(parts, 1), cols_op.at[v])
            block[pl.ds(q * half, half)] = res.reshape(half, height, PC)
            return carry

        lax.fori_loop(0, 2, cols_stage, 0)
        for e, c in ((0, 0), (1, pieces - 1)):
            x = jnp.concatenate([lines[k, c + 1] for k in range(terms)], 1)
            block[c] = block[c] - split_dot(x, edge_op.at[v, e])
        for c in range(pieces):
            cols = slice(c * PC, (c + 1) * PC)
            value = block[c]
            out_m[v, :, cols] = value.astype(BF)
            block[c] = value * inv_var[v, :, cols]
        add_up(v, 0, v == 0)
    send_sums(0)

    totals = []
    for which in (1, 0):
        def one(d, total):
            source = lax.rem(me + n - d, n)
            pltpu.make_async_copy(
                sums.at[which, 0], got.at[which, source], sum_recv.at[which, source]
            ).wait()
            return total + got[which, source]

        totals.append(lax.fori_loop(1, n, one, sums[which, me]))
    out_c[0] = totals[1] / jnp.maximum(totals[0], 1.0)

    for which in (0, 1):
        def done(d, carry):
            sum_copy(which, d).wait_send()
            return carry

        lax.fori_loop(1, n, done, 0)
    for v in range(early, visits):
        @pl.when(me < n - 1)
        def _():
            halo_copy(v, 0).wait_send()

        @pl.when(me > 0)
        def _():
            halo_copy(v, 1).wait_send()


def on_device(image, inv_var, shift, col_offset, psf_rows, psf_cols, placement):
    visits, height, width = image.shape
    n = lax.axis_size("tile")
    me = lax.axis_index("tile")
    terms = psf_rows.shape[1]
    pieces = width // PC
    early = visits - 1
    up = [(i, i + 1) for i in range(n - 1)]
    before = lax.ppermute(image[:early], "tile", up)
    after = lax.ppermute(image[:early], "tile", [(j, i) for i, j in up])
    row_tap = tap_weights(shift[:, 0])
    col_tap = tap_weights(shift[:, 1])
    rows_op = row_operator(row_tap, psf_rows, height, me, n)
    cols_op = col_operator(col_tap, col_offset, psf_cols)
    edge_op = edge_operator(col_tap, col_offset, psf_cols)
    hot = (placement == jnp.arange(n, dtype=jnp.int32)[None, :]).astype(F32).reshape(-1)
    vmem = pl.BlockSpec(memory_space=pltpu.VMEM)
    return pl.pallas_call(
        functools.partial(main_kernel, n, terms),
        out_shape=(
            jax.ShapeDtypeStruct((visits, height, width), BF),
            jax.ShapeDtypeStruct((1, height, PC), F32),
        ),
        in_specs=[vmem] * 7 + [pl.BlockSpec(memory_space=pltpu.SMEM)],
        out_specs=(vmem, vmem),
        scratch_shapes=[
            pltpu.VMEM((2, visits - early, height, width), F32),
            pltpu.VMEM((terms, pieces + 2, height, PC), F32),
            pltpu.VMEM((pieces, height, PC), F32),
            pltpu.VMEM((2, n, height, PC), F32),
            pltpu.VMEM((2, n, height, PC), F32),
            pltpu.SemaphoreType.DMA((2, visits - early)),
            pltpu.SemaphoreType.DMA((2, visits - early)),
            pltpu.SemaphoreType.DMA((2, n)),
            pltpu.SemaphoreType.DMA((2, n)),
        ],
        compiler_params=pltpu.CompilerParams(
            collective_id=0, has_side_effects=True, vmem_limit_bytes=48 * 1024 * 1024
        ),
    )(image, before, after, inv_var, rows_op, cols_op, edge_op, hot)


def solution(mesh):
    in_specs = (
        P(None, ("groups", "tile"), None),
        P(None, ("groups", "tile"), None),
        P("groups", None),
        P("groups"),
        P("groups", None, None),
        P("groups", None, None),
        P(("groups", "tile"), None),
    )
    out_specs = (P(None, ("groups", "tile"), None), P(("groups", "tile"), None, None))
    return jax.shard_map(
        on_device, mesh=mesh, in_specs=in_specs, out_specs=out_specs, check_vma=False
    )
```

```python
import functools

import jax
import jax.numpy as jnp
from jax import lax
from jax.experimental import pallas as pl
from jax.experimental.pallas import tpu as pltpu
from jax.sharding import PartitionSpec as P

PC = 128
LEAD = 20
BF = jnp.bfloat16
F32 = jnp.float32


def lanczos(values):
    return jnp.where(jnp.abs(values) < 3.0, jnp.sinc(values) * jnp.sinc(values / 3.0), 0.0)


def tap_weights(fraction):
    places = jnp.arange(-3, 4).astype(F32)
    weights = lanczos(places[None, :] + fraction[:, None])
    return weights / jnp.sum(weights, axis=1, keepdims=True)


def two_terms(x):
    high = x.astype(BF)
    return high, (x - high.astype(F32)).astype(BF)


def rounded_terms(x):
    high = lax.reduce_precision(x, exponent_bits=8, mantissa_bits=7)
    return high.astype(BF), (x - high).astype(BF)


def pick(weights, index):
    total = 0.0
    for t in range(weights.shape[1]):
        w = weights[:, t].reshape((-1,) + (1,) * (index.ndim - 1))
        total = total + jnp.where(index == t, w, 0.0)
    return total


def row_operator(row_tap, psf_rows, height, me, n):
    visits, terms, _ = psf_rows.shape
    i = jnp.arange(height, dtype=jnp.int32)[:, None, None]
    m = jnp.arange(height + 40, dtype=jnp.int32)[None, :, None]
    select = (i - m + 40 == jnp.arange(41, dtype=jnp.int32)[None, None, :]).astype(F32)
    band = jnp.einsum("vka,ima->vkim", psf_rows, select, precision=lax.Precision.HIGHEST)
    mi = jnp.arange(height + 40, dtype=jnp.int32)[:, None]
    ri = jnp.arange(3 * height, dtype=jnp.int32)[None, :]
    taps = pick(row_tap, (mi - ri + height - LEAD + 3)[None])
    row = me * height + mi - LEAD
    taps = jnp.where((row >= 0) & (row < n * height), taps, 0.0)
    full = jnp.einsum("vkim,vmr->vkir", band, taps, precision=lax.Precision.HIGHEST)
    full = full.reshape(visits, terms * height, 3 * height)
    high, low = rounded_terms(full)
    stacked = jnp.concatenate([high, high, low], axis=2)
    rows = -(-stacked.shape[1] // 16) * 16
    depth = -(-stacked.shape[2] // 256) * 256
    return jnp.pad(
        stacked, ((0, 0), (0, rows - stacked.shape[1]), (0, depth - stacked.shape[2]))
    )


def edge_operator(col_tap, col_offset, psf_cols):
    visits, terms, _ = psf_cols.shape
    m = jnp.arange(PC, dtype=jnp.int32)[:, None]
    j = jnp.arange(LEAD, dtype=jnp.int32)[None, :]
    place = jnp.stack([j - LEAD - m, PC + j - m])[None] - col_offset[:, None, None, None]
    taps = pick(col_tap, place + 3)
    jj = jnp.arange(LEAD, dtype=jnp.int32)[:, None]
    o = jnp.arange(PC, dtype=jnp.int32)[None, :]
    index = jnp.stack([o - jj + 40, o - PC - jj + 20])
    select = (index[..., None] == jnp.arange(41, dtype=jnp.int32)).astype(F32)
    psf = jnp.einsum("vkb,ejob->vkejo", psf_cols, select, precision=lax.Precision.HIGHEST)
    full = jnp.einsum("vemj,vkejo->vekmo", taps, psf, precision=lax.Precision.HIGHEST)
    high, low = rounded_terms(full.reshape(visits, 2, terms * PC, PC))
    return jnp.concatenate([high, low], axis=3)


def band_kernel(terms, c_ref, out_ref):
    for k in range(terms):
        row = jnp.broadcast_to(c_ref[0, k : k + 1, :], (PC, 2 * PC))
        turned = pltpu.roll(row, 0, 1, stride=1, stride_axis=0)
        m = lax.broadcasted_iota(jnp.int32, (PC, PC), 0)
        o = lax.broadcasted_iota(jnp.int32, (PC, PC), 1)
        far = turned[:, PC:]
        for d, part in enumerate(
            [jnp.where(o < m, far, 0.0), turned[:, :PC], jnp.where(o > m, far, 0.0)]
        ):
            high = part.astype(BF)
            low = (part - high.astype(F32)).astype(BF)
            start = (3 * k + d) * PC
            out_ref[0, start : start + PC, :PC] = high
            out_ref[0, start : start + PC, PC:] = low


def col_operator(col_tap, col_offset, psf_cols):
    visits, terms, _ = psf_cols.shape
    b = jnp.arange(41, dtype=jnp.int32)[:, None]
    lane = jnp.arange(2 * PC, dtype=jnp.int32)[None, :]
    signed = jnp.where(lane < PC, lane, lane - 2 * PC)
    spread = pick(col_tap, (signed - b + LEAD + 3)[None] - col_offset[:, None, None])
    line = jnp.einsum("vkb,vbl->vkl", psf_cols, spread, precision=lax.Precision.HIGHEST)
    return pl.pallas_call(
        functools.partial(band_kernel, terms),
        grid=(visits,),
        in_specs=[pl.BlockSpec((1, terms, 2 * PC), lambda v: (v, 0, 0))],
        out_specs=pl.BlockSpec((1, terms * 3 * PC, 2 * PC), lambda v: (v, 0, 0)),
        out_shape=jax.ShapeDtypeStruct((visits, terms * 3 * PC, 2 * PC), BF),
    )(line)


def split_dot(x, w_ref):
    high, low = two_terms(x)
    wide = jnp.dot(high, w_ref[...], preferred_element_type=F32)
    narrow = jnp.dot(low, w_ref[:, :PC], preferred_element_type=F32)
    return wide[:, :PC] + wide[:, PC:] + narrow


def main_kernel(
    n, terms, image, before, after, inv_var, rows_op, cols_op, edge_op, hot, out_m, out_c,
    halo, lines, block, sums, got, halo_send, halo_recv, sum_send, sum_recv,
):
    visits, height, width = image.shape
    pieces = width // PC
    early = before.shape[0]
    me = lax.axis_index("tile")

    barrier = pltpu.get_barrier_semaphore()

    def greet(d, carry):
        pl.semaphore_signal(
            barrier, inc=1, device_id={"tile": lax.rem(me + d, n)},
            device_id_type=pl.DeviceIdType.MESH,
        )
        return carry

    lax.fori_loop(1, n, greet, 0)
    pl.semaphore_wait(barrier, n - 1)

    def halo_copy(v, side):
        other = me + 1 if side == 0 else me - 1
        return pltpu.make_async_remote_copy(
            src_ref=image.at[v], dst_ref=halo.at[side, v - early],
            send_sem=halo_send.at[side, v - early], recv_sem=halo_recv.at[side, v - early],
            device_id={"tile": other}, device_id_type=pl.DeviceIdType.MESH,
        )

    for v in range(early, visits):
        @pl.when(me < n - 1)
        def _():
            halo_copy(v, 0).start()

        @pl.when(me > 0)
        def _():
            halo_copy(v, 1).start()

    @pl.when(me == 0)
    def _():
        halo[0] = jnp.zeros_like(halo[0])

    @pl.when(me == n - 1)
    def _():
        halo[1] = jnp.zeros_like(halo[1])

    def add_up(v, which, first):
        def owner(p, carry):
            total = jnp.zeros((height, PC), F32) if first else sums[which, p]
            for c in range(pieces):
                total = total + hot[(v * pieces + c) * n + p] * block[c]
            sums[which, p] = total
            return carry

        lax.fori_loop(0, n, owner, 0)

    def sum_copy(which, d):
        return pltpu.make_async_remote_copy(
            src_ref=sums.at[which, lax.rem(me + d, n)], dst_ref=got.at[which, me],
            send_sem=sum_send.at[which, d], recv_sem=sum_recv.at[which, me],
            device_id={"tile": lax.rem(me + d, n)}, device_id_type=pl.DeviceIdType.MESH,
        )

    def send_sums(which):
        def one(d, carry):
            sum_copy(which, d).start()
            return carry

        lax.fori_loop(1, n, one, 0)

    for v in range(visits):
        for c in range(pieces):
            block[c] = inv_var[v, :, c * PC : (c + 1) * PC]
        add_up(v, 1, v == 0)
    send_sums(1)

    for k in range(terms):
        lines[k, 0] = jnp.zeros((height, PC), F32)
        lines[k, pieces + 1] = jnp.zeros((height, PC), F32)

    depth = rows_op.shape[2]
    step = 4
    for v in range(visits):
        if v < early:
            above, below = before.at[v], after.at[v]
        else:
            above, below = halo.at[0, v - early], halo.at[1, v - early]

            @pl.when(me > 0)
            def _():
                pltpu.make_async_copy(image.at[v], above, halo_recv.at[0, v - early]).wait()

            @pl.when(me < n - 1)
            def _():
                pltpu.make_async_copy(image.at[v], below, halo_recv.at[1, v - early]).wait()

        def rows_stage(q, carry, above=above, below=below, v=v):
            cols = pl.ds(pl.multiple_of(q * (step * PC), step * PC), step * PC)
            x = jnp.concatenate([above[:, cols], image[v, :, cols], below[:, cols]], 0)
            high = x.astype(BF).astype(F32)
            rest = jnp.zeros((depth - 9 * height, step * PC), F32)
            stacked = jnp.concatenate([high, x - high, high, rest], 0).astype(BF)
            y = jnp.dot(rows_op[v], stacked, preferred_element_type=F32)
            for k in range(terms):
                for s in range(step):
                    lines[k, q * step + s + 1] = y[
                        k * height : (k + 1) * height, s * PC : (s + 1) * PC
                    ]
            return carry

        lax.fori_loop(0, pieces // step, rows_stage, 0)

        half = pieces // 2

        def cols_stage(q, carry):
            parts = [
                lines[k, pl.ds(q * half + d, half)].reshape(half * height, PC)
                for k in range(terms)
                for d in range(3)
            ]
            res = split_dot(jnp.concatenate(parts, 1), cols_op.at[v])
            block[pl.ds(q * half, half)] = res.reshape(half, height, PC)
            return carry

        lax.fori_loop(0, 2, cols_stage, 0)
        for e, c in ((0, 0), (1, pieces - 1)):
            x = jnp.concatenate([lines[k, c + 1] for k in range(terms)], 1)
            block[c] = block[c] - split_dot(x, edge_op.at[v, e])
        for c in range(pieces):
            cols = slice(c * PC, (c + 1) * PC)
            value = block[c]
            out_m[v, :, cols] = value.astype(BF)
            block[c] = value * inv_var[v, :, cols]
        add_up(v, 0, v == 0)
    send_sums(0)

    totals = []
    for which in (1, 0):
        def one(d, total):
            source = lax.rem(me + n - d, n)
            pltpu.make_async_copy(
                sums.at[which, 0], got.at[which, source], sum_recv.at[which, source]
            ).wait()
            return total + got[which, source]

        totals.append(lax.fori_loop(1, n, one, sums[which, me]))
    out_c[0] = totals[1] / jnp.maximum(totals[0], 1.0)

    for which in (0, 1):
        def done(d, carry):
            sum_copy(which, d).wait_send()
            return carry

        lax.fori_loop(1, n, done, 0)
    for v in range(early, visits):
        @pl.when(me < n - 1)
        def _():
            halo_copy(v, 0).wait_send()

        @pl.when(me > 0)
        def _():
            halo_copy(v, 1).wait_send()


def on_device(image, inv_var, shift, col_offset, psf_rows, psf_cols, placement):
    visits, height, width = image.shape
    n = lax.axis_size("tile")
    me = lax.axis_index("tile")
    terms = psf_rows.shape[1]
    pieces = width // PC
    early = max(1, visits // 4)
    up = [(i, i + 1) for i in range(n - 1)]
    before = lax.ppermute(image[:early], "tile", up)
    after = lax.ppermute(image[:early], "tile", [(j, i) for i, j in up])
    row_tap = tap_weights(shift[:, 0])
    col_tap = tap_weights(shift[:, 1])
    rows_op = row_operator(row_tap, psf_rows, height, me, n)
    cols_op = col_operator(col_tap, col_offset, psf_cols)
    edge_op = edge_operator(col_tap, col_offset, psf_cols)
    hot = (placement == jnp.arange(n, dtype=jnp.int32)[None, :]).astype(F32).reshape(-1)
    vmem = pl.BlockSpec(memory_space=pltpu.VMEM)
    return pl.pallas_call(
        functools.partial(main_kernel, n, terms),
        out_shape=(
            jax.ShapeDtypeStruct((visits, height, width), BF),
            jax.ShapeDtypeStruct((1, height, PC), F32),
        ),
        in_specs=[vmem] * 7 + [pl.BlockSpec(memory_space=pltpu.SMEM)],
        out_specs=(vmem, vmem),
        scratch_shapes=[
            pltpu.VMEM((2, visits - early, height, width), F32),
            pltpu.VMEM((terms, pieces + 2, height, PC), F32),
            pltpu.VMEM((pieces, height, PC), F32),
            pltpu.VMEM((2, n, height, PC), F32),
            pltpu.VMEM((2, n, height, PC), F32),
            pltpu.SemaphoreType.DMA((2, visits - early)),
            pltpu.SemaphoreType.DMA((2, visits - early)),
            pltpu.SemaphoreType.DMA((2, n)),
            pltpu.SemaphoreType.DMA((2, n)),
        ],
        compiler_params=pltpu.CompilerParams(
            collective_id=0, has_side_effects=True, vmem_limit_bytes=48 * 1024 * 1024
        ),
    )(image, before, after, inv_var, rows_op, cols_op, edge_op, hot)


def solution(mesh):
    in_specs = (
        P(None, ("groups", "tile"), None),
        P(None, ("groups", "tile"), None),
        P("groups", None),
        P("groups"),
        P("groups", None, None),
        P("groups", None, None),
        P(("groups", "tile"), None),
    )
    out_specs = (P(None, ("groups", "tile"), None), P(("groups", "tile"), None, None))
    return jax.shard_map(
        on_device, mesh=mesh, in_specs=in_specs, out_specs=out_specs, check_vma=False
    )
```
